32 devices in a mesh: groups: 2 (over x), wide: 16 (over z, y, core).
Axes of the slice: x: 2, y: 2, z: 4, core: 2. Of those that a mesh axis runs over, the one named last changes fastest.
Arguments:
- kernel_coarse: bfloat16 [128, 32, 2048], P(('groups', 'wide')), parts along dimension 0, may hold values from -6 to 6
- row_coeffs: bfloat16 [2048, 2, 1024], P(('groups', 'wide')), parts along dimension 0, may hold values from -1 to 1
- col_coeffs: bfloat16 [32, 1024], P('groups', 'wide'), parts along dimension 0, may hold values from -1 to 1
- column_coarse: int32 [32], P('groups'), parts along dimension 0, may hold values from 0 to 63
- row_coarse: int32 [2048, 2], P(('groups', 'wide')), parts along dimension 0, may hold values from 0 to 63, as said below
Outputs:
- hamiltonian: float32 [2048, 32, 512], P(('groups', 'wide')), parts along dimension 0
The draws below stay inside these ranges and needn't reach their ends.
There are 2 independent parts, one for each index of `groups`. The reference program is written for one: setup_inputs(seed, part) draws one part's arguments, and reference() takes and returns one part's arrays. A program takes and returns all parts, laid end to end along the dimension named above; each array names one. Nothing has to cross between parts.
Inputs may be any that keep to these rules, and one draw needn't show every extreme that they name: `row_coarse`: coarse row c belongs to owner device c // 4. In each aligned block of 64 fine rows, each owner device is named by either none or exactly 16 of the block's 2 * 64 entries. The 2 entries of one fine row differ.
All inputs are finite; a program needn't handle non-finite values.
Results may differ from the reference program's by a relative error of at most 0.005.
Values may be sent and summed in bfloat16 or wider, within the bound.
A program may use at most 64 MiB of HBM per device.

```python
import jax
import jax.numpy as jnp
from jax import lax

PAIRS = 32
NB = 2
NCC = 64
NFC = 16
CO_DEV = 4
F_DEV = 64
NCO = 64
NF = 1024
CAP = 16
N_WIDE = 16


def draw_row_coarse(key, part):
    key = jax.random.fold_in(key, 11)
    ref_count = F_DEV * NB

    def draw_block(block_key):
        key_perm, key_first, key_offset, key_spread = jax.random.split(block_key, 4)
        owner_perm = jax.random.permutation(key_perm, N_WIDE)
        spread = jax.random.permutation(key_spread, ref_count)
        owner_dev = owner_perm[spread // CAP]
        first_nb = jax.random.randint(key_first, (F_DEV, 1), 0, CO_DEV)
        offset_nb = jax.random.randint(key_offset, (F_DEV, NB - 1), 1, CO_DEV)
        local_rows = jnp.concatenate([first_nb, (first_nb + offset_nb) % CO_DEV], axis=1).reshape(ref_count)
        return (owner_dev * CO_DEV + local_rows).astype(jnp.int32).reshape(F_DEV, NB)
    block_keys = jax.random.split(key, N_WIDE)
    return jax.vmap(draw_block)(block_keys).reshape(NF, NB)


def plant(entries, key, smallest, largest):
    place = [jax.random.randint(jax.random.fold_in(key, axis), (), 0, length) for axis, length in enumerate(entries.shape)]
    main_axis = entries.shape.index(max(entries.shape))
    neighbour = place[:main_axis] + [(place[main_axis] + 1) % entries.shape[main_axis]] + place[main_axis + 1:]
    return entries.at[tuple(place)].set(smallest).at[tuple(neighbour)].set(largest)


def level_of(own_key, shape, pieces, smallest, high):
    level = 1.0
    for dim, blocks in pieces:
        heights = jax.random.uniform(jax.random.fold_in(jax.random.fold_in(own_key, 6), dim), (blocks,), jnp.float32, smallest / len(pieces), high / len(pieces))
        level = level * jnp.repeat(jnp.exp(heights), shape[dim] // blocks).reshape((-1,) + (1,) * (len(shape) - 1 - dim))
    return level


def bell_draw(key, shape, scale, most, cuts=(), kind=jnp.bfloat16):
    loudness = level_of(key, shape, cuts, -0.22, 0.18) if cuts else 1.0
    array = jax.random.normal(key, shape, jnp.float32) * scale * loudness
    return jnp.minimum(jnp.maximum(array, -most), most).astype(kind)


def setup_inputs(seed: int = 0, part: int = 0) -> dict:
    seeds = jax.random.split(jax.random.key(seed), 6)
    part_keys = jax.random.split(jax.random.fold_in(seeds[5], part), 6)
    kernel_coarse = bell_draw(part_keys[0], (NCO, PAIRS, NCC * PAIRS), 1.0, 6.0, ((0, 16),))
    row_coeffs = bell_draw(part_keys[1], (NF, NB, PAIRS * PAIRS), PAIRS ** -0.5, 1.0, ((0, 16),))
    col_coeffs = bell_draw(part_keys[2], (NFC, PAIRS * PAIRS), PAIRS ** -0.5, 1.0, ((1, 16),))
    column_coarse = plant(jax.random.randint(part_keys[3], (NFC,), 0, NCC), jax.random.fold_in(part_keys[3], 1), 0, NCC - 1).astype(jnp.int32)
    row_coarse = draw_row_coarse(jax.random.fold_in(jax.random.fold_in(seeds[5], part), 71), part)
    return dict(kernel_coarse=kernel_coarse, row_coeffs=row_coeffs, col_coeffs=col_coeffs, column_coarse=column_coarse, row_coarse=row_coarse)


def expand_panel(col_coeffs, column_coarse):
    onehot = (column_coarse[None, :] == jnp.arange(NCC, dtype=jnp.int32)[:, None]).astype(jnp.float32)
    col_mats = jnp.transpose(col_coeffs.astype(jnp.float32).reshape(NFC, PAIRS, PAIRS), (1, 0, 2))
    col_panel = onehot[:, None, :, None] * col_mats[None, :, :, :]
    return col_panel.reshape(NCC * PAIRS, NFC * PAIRS).astype(jnp.bfloat16)


def reference(kernel_coarse, row_coeffs, col_coeffs, column_coarse, row_coarse):
    col_panel = expand_panel(col_coeffs, column_coarse)
    expanded = jnp.dot(kernel_coarse.reshape(NCO * PAIRS, NCC * PAIRS), col_panel, preferred_element_type=jnp.float32)
    expanded = expanded.astype(jnp.bfloat16).reshape(NCO, PAIRS, NFC * PAIRS)

    def fine_block(block_args):
        coeff_block, pick_block = block_args
        chosen = expanded[pick_block].astype(jnp.float32)
        left_mats = coeff_block.reshape(F_DEV, NB, PAIRS, PAIRS).astype(jnp.float32)
        tile_terms = jnp.einsum("fnba,fnbx->fnax", left_mats, chosen).astype(jnp.bfloat16)
        return jnp.sum(tile_terms.astype(jnp.float32), axis=1)

    stacked = lax.map(fine_block, (row_coeffs.reshape(N_WIDE, F_DEV, NB, PAIRS * PAIRS), row_coarse.reshape(N_WIDE, F_DEV, NB)))
    return stacked.reshape(NF, PAIRS, NFC * PAIRS)
```

```python
import functools

import jax
import jax.numpy as jnp
from jax import lax
from jax.experimental import pallas as pl
from jax.experimental.pallas import tpu as pltpu
from jax.sharding import PartitionSpec as P

PAIR = 32
NCC = 64


def expand_panel(col_coeffs, column_coarse):
    fine_cols = column_coarse.shape[0]
    onehot = (column_coarse[None, :] == jnp.arange(NCC, dtype=jnp.int32)[:, None]).astype(jnp.bfloat16)
    col_mats = jnp.transpose(col_coeffs.reshape(fine_cols, PAIR, PAIR), (1, 0, 2))
    col_panel = onehot[:, None, :, None] * col_mats[None, :, :, :]
    return col_panel.reshape(NCC * PAIR, fine_cols * PAIR)


def fine_kernel(per_step, picks_ref, expanded_ref, left_ref, out_ref):
    step = pl.program_id(0)
    for u in range(per_step):
        row = step * per_step + u
        first = pl.multiple_of(picks_ref[2 * row] * PAIR, PAIR)
        second = pl.multiple_of(picks_ref[2 * row + 1] * PAIR, PAIR)
        chosen = jnp.concatenate(
            [expanded_ref[pl.ds(first, PAIR), :], expanded_ref[pl.ds(second, PAIR), :]], axis=0
        )
        out_ref[u] = jnp.dot(
            left_ref[u * PAIR : (u + 1) * PAIR, :], chosen, preferred_element_type=jnp.float32
        )


def fine_rows_of(picks, expanded, left):
    fine_rows = picks.shape[0] // 2
    width = expanded.shape[1]
    per_step = 8
    return pl.pallas_call(
        functools.partial(fine_kernel, per_step),
        grid_spec=pltpu.PrefetchScalarGridSpec(
            num_scalar_prefetch=1,
            grid=(fine_rows // per_step,),
            in_specs=[
                pl.BlockSpec(memory_space=pltpu.VMEM),
                pl.BlockSpec((per_step * PAIR, 2 * PAIR), lambda s, picks: (s, 0)),
            ],
            out_specs=pl.BlockSpec((per_step, PAIR, width), lambda s, picks: (s, 0, 0)),
        ),
        out_shape=jax.ShapeDtypeStruct((fine_rows, PAIR, width), jnp.float32),
        compiler_params=pltpu.CompilerParams(vmem_limit_bytes=48 * 1024 * 1024),
        name="fine_rows",
    )(picks, expanded, left)


def per_device(kernel_coarse, row_coeffs, col_coeffs, column_coarse, row_coarse):
    whole_cols = lax.all_gather(col_coeffs, "wide", axis=1, tiled=True)
    col_panel = expand_panel(whole_cols, column_coarse)
    owned = kernel_coarse.shape[0] * PAIR
    expanded = jnp.dot(
        kernel_coarse.reshape(owned, -1), col_panel, preferred_element_type=jnp.float32
    ).astype(jnp.bfloat16)
    expanded = lax.all_gather(expanded, "wide", axis=0, tiled=True)
    fine_rows = row_coeffs.shape[0]
    left = row_coeffs.reshape(fine_rows, 2, PAIR, PAIR).transpose(0, 3, 1, 2)
    left = left.reshape(fine_rows * PAIR, 2 * PAIR)
    return fine_rows_of(row_coarse.reshape(-1), expanded, left)


def solution(mesh):
    in_specs = (
        P(("groups", "wide"), None, None),
        P(("groups", "wide"), None, None),
        P("groups", "wide"),
        P("groups"),
        P(("groups", "wide"), None),
    )
    out_specs = P(("groups", "wide"), None, None)
    return jax.shard_map(
        per_device, mesh=mesh, in_specs=in_specs, out_specs=out_specs, check_vma=False
    )
```

```python
import functools

import jax
import jax.numpy as jnp
from jax import lax
from jax.experimental import pallas as pl
from jax.experimental.pallas import tpu as pltpu
from jax.sharding import PartitionSpec as P

PAIR = 32
MESH = pl.DeviceIdType.MESH


def fine_kernel(per_step, picks_ref, expanded_ref, left_ref, out_ref):
    step = pl.program_id(0)
    for u in range(per_step):
        row = step * per_step + u
        first = pl.multiple_of(picks_ref[2 * row] * PAIR, PAIR)
        second = pl.multiple_of(picks_ref[2 * row + 1] * PAIR, PAIR)
        chosen = jnp.concatenate(
            [expanded_ref[pl.ds(first, PAIR), :], expanded_ref[pl.ds(second, PAIR), :]], axis=0
        )
        out_ref[u] = jnp.dot(
            left_ref[u * PAIR : (u + 1) * PAIR, :], chosen, preferred_element_type=jnp.float32
        )


def fine_rows_of(picks, expanded, left):
    fine_rows = picks.shape[0] // 2
    width = expanded.shape[1]
    per_step = 8
    return pl.pallas_call(
        functools.partial(fine_kernel, per_step),
        grid_spec=pltpu.PrefetchScalarGridSpec(
            num_scalar_prefetch=1,
            grid=(fine_rows // per_step,),
            in_specs=[
                pl.BlockSpec(memory_space=pltpu.VMEM),
                pl.BlockSpec((per_step * PAIR, 2 * PAIR), lambda s, picks: (s, 0)),
            ],
            out_specs=pl.BlockSpec((per_step, PAIR, width), lambda s, picks: (s, 0, 0)),
        ),
        out_shape=jax.ShapeDtypeStruct((fine_rows, PAIR, width), jnp.float32),
        compiler_params=pltpu.CompilerParams(vmem_limit_bytes=48 * 1024 * 1024),
        name="fine_rows",
    )(picks, expanded, left)


def ring_place(chip, chips):
    rung, side = lax.div(chip, 2), lax.rem(chip, 2)
    return (1 - side) * rung + side * (chips - 1 - rung)


def chip_at(place, chips):
    place = lax.rem(place + 2 * chips, chips)
    side = lax.div(place, chips // 2)
    return (1 - side) * (2 * place) + side * (2 * (chips - 1 - place) + 1)


def iota(shape, dim):
    return lax.broadcasted_iota(jnp.int32, shape, dim)


def ones_where(mask):
    return jnp.where(mask, 1.0, 0.0).astype(jnp.bfloat16)


def pick_kernel(column_ref, coarse_ref, picked_ref):
    lane_gap = iota((128, 128), 0) - iota((128, 128), 1)
    lane_group = lax.div(iota((128, 128), 1), PAIR)
    for block in range(picked_ref.shape[1] // 128):
        sources, moves = [], []
        for j in range(4):
            coarse = column_ref[4 * block + j]
            wide_block = lax.div(coarse, 4)
            offset = (coarse - 4 * wide_block - j) * PAIR
            sources.append(coarse_ref[:, pl.ds(pl.multiple_of(wide_block * 128, 128), 128)])
            moves.append(ones_where((lane_group == j) & (lane_gap == offset)))
        picked_ref[:, block * 128 : (block + 1) * 128] = jnp.dot(
            jnp.concatenate(sources, axis=1),
            jnp.concatenate(moves, axis=0),
            preferred_element_type=jnp.float32,
        ).astype(jnp.bfloat16)

def pick(column_coarse, coarse):
    return pl.pallas_call(
        pick_kernel,
        out_shape=jax.ShapeDtypeStruct(
            (coarse.shape[0], column_coarse.shape[0] * PAIR), jnp.bfloat16
        ),
        in_specs=[pl.BlockSpec(memory_space=pltpu.SMEM), pl.BlockSpec(memory_space=pltpu.VMEM)],
        out_specs=pl.BlockSpec(memory_space=pltpu.VMEM),
        name="pick",
    )(column_coarse, coarse)


def exchange_kernel(
    n, piece, block_ref, cols_ref, expanded_ref,
    picked, cols, right0, right1, spread,
    cols_send, cols_recv, ring_send, ring_recv, twin_send, twin_recv,
):
    me = lax.axis_index("wide")
    chips = n // 2
    core = lax.rem(me, 2)
    place = ring_place(lax.div(me, 2), chips)
    twin = me + 1 - 2 * core
    ahead = 2 * chip_at(place + 1, chips) + core
    behind = 2 * chip_at(place - 1, chips) + core
    targets = (ahead, behind)
    rows, width = picked.shape[1], picked.shape[2]
    half = rows // 2
    fine_cols = width // PAIR
    far = chips // 2

    def peer(k):
        return lax.rem(me + k, n)

    barrier = pltpu.get_barrier_semaphore()

    def greet(k, carry):
        pl.semaphore_signal(barrier, inc=1, device_id={"wide": peer(k)}, device_id_type=MESH)
        return carry

    lax.fori_loop(1, n, greet, 0)

    picked[me] = block_ref[...]
    cols[pl.ds(pl.multiple_of(me * fine_cols, fine_cols), fine_cols), :] = cols_ref[...]

    pl.semaphore_wait(barrier, n - 1)

    def ring_copy(way, dist, part, source):
        spot = picked.at[source, pl.ds(part * half, half)]
        return pltpu.make_async_remote_copy(
            src_ref=spot, dst_ref=spot,
            send_sem=ring_send.at[way, dist - 1, part],
            recv_sem=ring_recv.at[way, dist - 1, part],
            device_id={"wide": targets[way]}, device_id_type=MESH,
        )

    def twin_copy(way, dist, part, source):
        spot = picked.at[source, pl.ds(part * half, half)]
        return pltpu.make_async_remote_copy(
            src_ref=spot, dst_ref=spot,
            send_sem=twin_send.at[way, dist, part],
            recv_sem=twin_recv.at[way, dist, part],
            device_id={"wide": twin}, device_id_type=MESH,
        )

    def cols_copy(k, source):
        spot = cols.at[pl.ds(pl.multiple_of(source * fine_cols, fine_cols), fine_cols), :]
        return pltpu.make_async_remote_copy(
            src_ref=spot, dst_ref=spot,
            send_sem=cols_send.at[k - 1], recv_sem=cols_recv.at[k - 1],
            device_id={"wide": peer(k)}, device_id_type=MESH,
        )

    sent = []

    def start(copy):
        copy.start()
        sent.append(copy)

    for turn in range(2):
        for way in range(2):
            if far > 1 or (turn ^ way) == way:
                start(ring_copy(way, 1, turn ^ way, me))

    def send_cols(k, carry):
        cols_copy(k, me).start()
        return carry

    lax.fori_loop(1, n, send_cols, 0)
    for part in range(2):
        start(twin_copy(0, 0, part, me))

    def wait_cols():
        def wait_one(k, carry):
            cols_copy(k, lax.rem(me - k + n, n)).wait_recv()
            return carry

        lax.fori_loop(1, n, wait_one, 0)

    groups = max(piece, PAIR) // min(piece, PAIR)

    def spread_cols():
        lane, target = iota((128, width), 0), lax.rem(iota((128, width), 1), PAIR)
        for g in range(groups):
            if piece >= PAIR:
                take = lane == PAIR * g + target
            else:
                take = (target == piece * g + lane) & (lane < piece)
            spread[g] = jnp.dot(
                cols[...], ones_where(take), preferred_element_type=jnp.float32
            ).astype(jnp.bfloat16)

    def form_right(side, right):
        shape = (width // 2, n * fine_cols)
        row, col = iota(shape, 0) + side * (width // 2), iota(shape, 1)
        fine, pair = lax.div(row, PAIR), lax.rem(row, PAIR)
        device, fine_from = lax.div(col, fine_cols), lax.rem(col, fine_cols)
        total = None
        for g in range(groups):
            if piece >= PAIR:
                take = (fine == fine_from) & (pair == groups * device + g)
            else:
                take = (fine == fine_from) & (device == groups * pair + g)
            term = jnp.dot(
                ones_where(take),
                spread[g, :, side * (width // 2) : (side + 1) * (width // 2)],
                preferred_element_type=jnp.float32,
            )
            total = term if total is None else total + term
        square = (width // 2, width // 2)
        same = lax.div(iota(square, 0), PAIR) == lax.div(iota(square, 1), PAIR)
        right[...] = jnp.where(same, total, 0.0).astype(jnp.bfloat16)

    def multiply(source, part):
        block = picked[source, pl.ds(part * half, half), :]
        at = pl.ds(pl.multiple_of(source * rows + part * half, half), half)
        for side, right in enumerate((right0, right1)):
            span = slice(side * (width // 2), (side + 1) * (width // 2))
            expanded_ref[at, span] = jnp.dot(
                block[:, span], right[...], preferred_element_type=jnp.float32
            ).astype(jnp.bfloat16)

    def own_work():
        multiply(me, 0)
        multiply(me, 1)

    def twin_work(way, dist, part, source):
        twin_copy(way, dist, part, source).wait_recv()
        multiply(source, part)

    def first_cols():
        wait_cols()
        spread_cols()

    work = [
        first_cols,
        functools.partial(form_right, 0, right0),
        functools.partial(form_right, 1, right1),
        own_work,
        functools.partial(twin_work, 0, 0, 0, twin),
        functools.partial(twin_work, 0, 0, 1, twin),
    ]
    for dist in range(1, far + 1):
        for turn in range(2):
            due = []
            for way in range(2):
                part = turn ^ way
                if dist == far and part != way:
                    continue
                chip = chip_at(place + (dist if way else -dist), chips)
                mine, other = 2 * chip + core, 2 * chip + 1 - core
                ring_copy(way, dist, part, mine).wait_recv()
                if dist + 1 < far or (dist + 1 == far and part == way):
                    start(ring_copy(way, dist + 1, part, mine))
                start(twin_copy(way, dist, part, mine))
                due.append(functools.partial(multiply, mine, part))
                due.append(functools.partial(twin_work, way, dist, part, other))
            own, theirs = due[0::2], due[1::2]
            for _ in range(4 if work else 0):
                if work:
                    work.pop(0)()
            work += own + theirs
    for step in work:
        step()
    for copy in sent:
        copy.wait_send()

    def wait_sent(k, carry):
        cols_copy(k, me).wait_send()
        return carry

    lax.fori_loop(1, n, wait_sent, 0)


def exchange(block, cols, n, piece):
    rows, width = block.shape
    fine_cols = cols.shape[0]
    far = n // 4
    groups = max(piece, PAIR) // min(piece, PAIR)
    total = n * rows * width * 2
    return pl.pallas_call(
        functools.partial(exchange_kernel, n, piece),
        out_shape=jax.ShapeDtypeStruct((n * rows, width), jnp.bfloat16),
        in_specs=[
            pl.BlockSpec(memory_space=pltpu.VMEM),
            pl.BlockSpec(memory_space=pltpu.VMEM),
        ],
        out_specs=pl.BlockSpec(memory_space=pltpu.VMEM),
        scratch_shapes=[
            pltpu.VMEM((n, rows, width), jnp.bfloat16),
            pltpu.VMEM((n * fine_cols, 128), jnp.bfloat16),
            pltpu.VMEM((width // 2, width // 2), jnp.bfloat16),
            pltpu.VMEM((width // 2, width // 2), jnp.bfloat16),
            pltpu.VMEM((groups, n * fine_cols, width), jnp.bfloat16),
            pltpu.SemaphoreType.DMA((n - 1,)),
            pltpu.SemaphoreType.DMA((n - 1,)),
            pltpu.SemaphoreType.DMA((2, far, 2)),
            pltpu.SemaphoreType.DMA((2, far, 2)),
            pltpu.SemaphoreType.DMA((2, far + 1, 2)),
            pltpu.SemaphoreType.DMA((2, far + 1, 2)),
        ],
        compiler_params=pltpu.CompilerParams(
            collective_id=0, has_side_effects=True, vmem_limit_bytes=2 * total + 12 * 1024 * 1024 + n * 64 * 1024
        ),
        name="exchange",
    )(block, cols)


def per_device(kernel_coarse, row_coeffs, col_coeffs, column_coarse, row_coarse):
    n = lax.axis_size("wide")
    piece = col_coeffs.shape[1]
    cols = jnp.pad(col_coeffs, ((0, 0), (0, 128 - piece)))
    coarse = kernel_coarse.reshape(kernel_coarse.shape[0] * PAIR, -1)
    expanded = exchange(pick(column_coarse, coarse), cols, n, piece)
    fine_rows = row_coeffs.shape[0]
    left = row_coeffs.reshape(fine_rows, 2, PAIR, PAIR).transpose(0, 3, 1, 2)
    left = left.reshape(fine_rows * PAIR, 2 * PAIR)
    return fine_rows_of(row_coarse.reshape(-1), expanded, left)


def solution(mesh):
    in_specs = (
        P(("groups", "wide"), None, None),
        P(("groups", "wide"), None, None),
        P("groups", "wide"),
        P("groups"),
        P(("groups", "wide"), None),
    )
    out_specs = P(("groups", "wide"), None, None)
    return jax.shard_map(
        per_device, mesh=mesh, in_specs=in_specs, out_specs=out_specs, check_vma=False
    )
```

```python
import functools

import jax
import jax.numpy as jnp
from jax import lax
from jax.experimental import pallas as pl
from jax.experimental.pallas import tpu as pltpu
from jax.sharding import PartitionSpec as P

PAIR = 32
COL_ROWS = 16
MESH = pl.DeviceIdType.MESH


def iota(shape, dim):
    return lax.broadcasted_iota(jnp.int32, shape, dim)


def ones_where(mask):
    return jnp.where(mask, 1.0, 0.0).astype(jnp.bfloat16)


def pick_kernel(column_ref, coarse_ref, picked_ref):
    lane_gap = iota((128, 128), 0) - iota((128, 128), 1)
    lane_group = lax.div(iota((128, 128), 1), PAIR)
    for block in range(picked_ref.shape[1] // 128):
        sources, moves = [], []
        for j in range(4):
            coarse = column_ref[4 * block + j]
            wide_block = lax.div(coarse, 4)
            offset = (coarse - 4 * wide_block - j) * PAIR
            sources.append(coarse_ref[:, pl.ds(pl.multiple_of(wide_block * 128, 128), 128)])
            moves.append(ones_where((lane_group == j) & (lane_gap == offset)))
        picked_ref[:, block * 128 : (block + 1) * 128] = jnp.dot(
            jnp.concatenate(sources, axis=1),
            jnp.concatenate(moves, axis=0),
            preferred_element_type=jnp.float32,
        ).astype(jnp.bfloat16)

def pick(column_coarse, coarse):
    return pl.pallas_call(
        pick_kernel,
        out_shape=jax.ShapeDtypeStruct(
            (coarse.shape[0], column_coarse.shape[0] * PAIR), jnp.bfloat16
        ),
        in_specs=[pl.BlockSpec(memory_space=pltpu.SMEM), pl.BlockSpec(memory_space=pltpu.VMEM)],
        out_specs=pl.BlockSpec(memory_space=pltpu.VMEM),
        name="pick",
    )(column_coarse, coarse)


def spread_cols(piece, gathered_ref, spread, right):
    n, fine_cols = gathered_ref.shape[0], COL_ROWS
    width = gathered_ref.shape[2]
    rows = gathered_ref.shape[1] - fine_cols
    side_width = right.shape[1]
    groups = spread.shape[0]
    cols = gathered_ref[:, rows:, 0:128].reshape(n * fine_cols, 128)
    lane, target = iota((128, width), 0), lax.rem(iota((128, width), 1), PAIR)
    for g in range(groups):
        if piece >= PAIR:
            take = lane == PAIR * g + target
        else:
            take = (target == piece * g + lane) & (lane < piece)
        spread[g] = jnp.dot(
            cols, ones_where(take), preferred_element_type=jnp.float32
        ).astype(jnp.bfloat16)
    for side in range(right.shape[0]):
        shape = (side_width, n * fine_cols)
        row, col = iota(shape, 0) + side * side_width, iota(shape, 1)
        fine, pair = lax.div(row, PAIR), lax.rem(row, PAIR)
        device, fine_from = lax.div(col, fine_cols), lax.rem(col, fine_cols)
        total = None
        for g in range(groups):
            if piece >= PAIR:
                take = (fine == fine_from) & (pair == groups * device + g)
            else:
                take = (fine == fine_from) & (device == groups * pair + g)
            term = jnp.dot(
                ones_where(take),
                spread[g, :, side * side_width : (side + 1) * side_width],
                preferred_element_type=jnp.float32,
            )
            total = term if total is None else total + term
        square = (side_width, side_width)
        same = lax.div(iota(square, 0), PAIR) == lax.div(iota(square, 1), PAIR)
        right[side] = jnp.where(same, total, 0.0).astype(jnp.bfloat16)


def fine_kernel(
    per_step, fine_rows, piece, picks_ref, gathered_ref, left_ref, out_ref, spread, right, half_done
):
    step = pl.program_id(0)
    owned = (gathered_ref.shape[1] - COL_ROWS) // PAIR
    side_width = right.shape[1]

    @pl.when(step == 0)
    def _():
        spread_cols(piece, gathered_ref, spread, right)

    def rows_of(coarse):
        owner = lax.div(coarse, owned)
        first = pl.multiple_of((coarse - owner * owned) * PAIR, PAIR)
        return gathered_ref[owner, pl.ds(first, PAIR), :]

    for u in range(per_step):
        row = step * per_step + u
        chosen = jnp.concatenate(
            [rows_of(picks_ref[row]), rows_of(picks_ref[fine_rows + row])], axis=0
        )
        half_done[u * PAIR : (u + 1) * PAIR, :] = jnp.dot(
            left_ref[u * PAIR : (u + 1) * PAIR, :], chosen, preferred_element_type=jnp.float32
        ).astype(jnp.bfloat16)
    for side in range(right.shape[0]):
        span = slice(side * side_width, (side + 1) * side_width)
        out_ref[:, :, span] = jnp.dot(
            half_done[:, span], right[side], preferred_element_type=jnp.float32
        ).reshape(per_step, PAIR, side_width)


def fine_rows_of(picks, gathered, left, piece):
    fine_rows = picks.shape[0] // 2
    n, width = gathered.shape[0], gathered.shape[2]
    per_step = 8
    groups = max(piece, PAIR) // min(piece, PAIR)
    return pl.pallas_call(
        functools.partial(fine_kernel, per_step, fine_rows, piece),
        grid_spec=pltpu.PrefetchScalarGridSpec(
            num_scalar_prefetch=1,
            grid=(fine_rows // per_step,),
            in_specs=[
                pl.BlockSpec(memory_space=pltpu.VMEM),
                pl.BlockSpec((per_step * PAIR, 2 * PAIR), lambda s, picks: (s, 0)),
            ],
            out_specs=pl.BlockSpec((per_step, PAIR, width), lambda s, picks: (s, 0, 0)),
            scratch_shapes=[
                pltpu.VMEM((groups, n * COL_ROWS, width), jnp.bfloat16),
                pltpu.VMEM((2, width // 2, width // 2), jnp.bfloat16),
                pltpu.VMEM((per_step * PAIR, width), jnp.bfloat16),
            ],
        ),
        out_shape=jax.ShapeDtypeStruct((fine_rows, PAIR, width), jnp.float32),
        compiler_params=pltpu.CompilerParams(
            vmem_limit_bytes=16 * 1024 * 1024 + n * 256 * 1024
        ),
        name="fine_rows",
    )(picks, gathered, left)


def ring_place(chip, chips):
    rung, side = lax.div(chip, 2), lax.rem(chip, 2)
    return (1 - side) * rung + side * (chips - 1 - rung)


def chip_at(place, chips):
    place = lax.rem(place + 2 * chips, chips)
    side = lax.div(place, chips // 2)
    return (1 - side) * (2 * place) + side * (2 * (chips - 1 - place) + 1)


def exchange_kernel(
    n, block_ref, cols_ref, gathered_ref, ring_send, ring_recv, twin_send, twin_recv
):
    me = lax.axis_index("wide")
    chips = n // 2
    core = lax.rem(me, 2)
    place = ring_place(lax.div(me, 2), chips)
    twin = me + 1 - 2 * core
    ahead = 2 * chip_at(place + 1, chips) + core
    behind = 2 * chip_at(place - 1, chips) + core
    targets = (ahead, behind)
    rows, width = block_ref.shape
    fine_cols, piece = cols_ref.shape
    parts = ((0, rows // 2), (rows // 2, rows // 2 + fine_cols))
    far = chips // 2

    barrier = pltpu.get_barrier_semaphore()
    for friend in (ahead, behind, twin):
        pl.semaphore_signal(barrier, inc=1, device_id={"wide": friend}, device_id_type=MESH)
    gathered_ref[me, 0:rows, :] = block_ref[...]
    gathered_ref[me, rows:, :] = jnp.concatenate(
        [cols_ref[...], jnp.zeros((fine_cols, width - piece), jnp.bfloat16)], axis=1
    )
    pl.semaphore_wait(barrier, 3)

    def copy_of(part, source, send, recv, target):
        spot = gathered_ref.at[source, pl.ds(*parts[part])]
        return pltpu.make_async_remote_copy(
            src_ref=spot, dst_ref=spot, send_sem=send, recv_sem=recv,
            device_id={"wide": target}, device_id_type=MESH,
        )

    def ring_copy(way, dist, part, source):
        at = (way, dist - 1, part)
        return copy_of(part, source, ring_send.at[at], ring_recv.at[at], targets[way])

    def twin_copy(way, dist, part, source):
        at = (way, dist, part)
        return copy_of(part, source, twin_send.at[at], twin_recv.at[at], twin)

    sent, coming = [], []

    def start(copy):
        copy.start()
        sent.append(copy)

    def goes(way, dist, part):
        return dist < far or (dist == far and part == way)

    for turn in range(2):
        for way in range(2):
            if goes(way, 1, turn ^ way):
                start(ring_copy(way, 1, turn ^ way, me))
    for part in range(2):
        start(twin_copy(0, 0, part, me))
        coming.append(twin_copy(0, 0, part, twin))
    for dist in range(1, far + 1):
        chip_of = [chip_at(place + (dist if way else -dist), chips) for way in range(2)]
        for turn in range(2):
            arrived = []
            for way in range(2):
                part = turn ^ way
                if not goes(way, dist, part):
                    continue
                mine = 2 * chip_of[way] + core
                ring_copy(way, dist, part, mine).wait_recv()
                if goes(way, dist + 1, part):
                    start(ring_copy(way, dist + 1, part, mine))
                arrived.append((way, part, mine))
            for way, part, mine in arrived:
                start(twin_copy(way, dist, part, mine))
                coming.append(twin_copy(way, dist, part, mine + 1 - 2 * core))
    for copy in coming:
        copy.wait_recv()
    for copy in sent:
        copy.wait_send()


def exchange(block, cols, n):
    rows, width = block.shape
    far = n // 4
    total = n * (rows + COL_ROWS) * width * 2
    return pl.pallas_call(
        functools.partial(exchange_kernel, n),
        out_shape=jax.ShapeDtypeStruct((n, rows + COL_ROWS, width), jnp.bfloat16),
        in_specs=[
            pl.BlockSpec(memory_space=pltpu.VMEM),
            pl.BlockSpec(memory_space=pltpu.VMEM),
        ],
        out_specs=pl.BlockSpec(memory_space=pltpu.VMEM),
        scratch_shapes=[
            pltpu.SemaphoreType.DMA((2, far, 2)),
            pltpu.SemaphoreType.DMA((2, far, 2)),
            pltpu.SemaphoreType.DMA((2, far + 1, 2)),
            pltpu.SemaphoreType.DMA((2, far + 1, 2)),
        ],
        compiler_params=pltpu.CompilerParams(
            collective_id=0, has_side_effects=True, vmem_limit_bytes=total + 6 * 1024 * 1024
        ),
        name="exchange",
    )(block, cols)


def per_device(kernel_coarse, row_coeffs, col_coeffs, column_coarse, row_coarse):
    n = lax.axis_size("wide")
    coarse = kernel_coarse.reshape(kernel_coarse.shape[0] * PAIR, -1)
    gathered = exchange(pick(column_coarse, coarse), col_coeffs, n)
    fine_rows = row_coeffs.shape[0]
    left = row_coeffs.reshape(fine_rows, 2, PAIR, PAIR).transpose(0, 3, 1, 2)
    left = left.reshape(fine_rows * PAIR, 2 * PAIR)
    return fine_rows_of(row_coarse.T.reshape(-1), gathered, left, col_coeffs.shape[1])


def solution(mesh):
    in_specs = (
        P(("groups", "wide"), None, None),
        P(("groups", "wide"), None, None),
        P("groups", "wide"),
        P("groups"),
        P(("groups", "wide"), None),
    )
    out_specs = P(("groups", "wide"), None, None)
    return jax.shard_map(
        per_device, mesh=mesh, in_specs=in_specs, out_specs=out_specs, check_vma=False
    )
```

```python
import functools

import jax
import jax.numpy as jnp
from jax import lax
from jax.experimental import pallas as pl
from jax.experimental.pallas import tpu as pltpu
from jax.sharding import PartitionSpec as P

PAIR = 32
SLOTS = 4
TEAM = 4
COL_ROWS = 16
MESH = pl.DeviceIdType.MESH


def iota(shape, dim):
    return lax.broadcasted_iota(jnp.int32, shape, dim)


def ones_where(mask):
    return jnp.where(mask, 1.0, 0.0).astype(jnp.bfloat16)


def pick_kernel(column_ref, coarse_ref, after_ref, picked_ref):
    lane_gap = iota((128, 128), 0) - iota((128, 128), 1)
    lane_group = lax.div(iota((128, 128), 1), PAIR)
    for block in range(picked_ref.shape[1] // 128):
        sources, moves = [], []
        for j in range(4):
            coarse = column_ref[4 * block + j]
            wide_block = lax.div(coarse, 4)
            offset = (coarse - 4 * wide_block - j) * PAIR
            sources.append(coarse_ref[:, pl.ds(pl.multiple_of(wide_block * 128, 128), 128)])
            moves.append(ones_where((lane_group == j) & (lane_gap == offset)))
        picked_ref[:, block * 128 : (block + 1) * 128] = jnp.dot(
            jnp.concatenate(sources, axis=1),
            jnp.concatenate(moves, axis=0),
            preferred_element_type=jnp.float32,
        ).astype(jnp.bfloat16)

def pick(column_coarse, coarse, after):
    return pl.pallas_call(
        pick_kernel,
        out_shape=jax.ShapeDtypeStruct(
            (coarse.shape[0], column_coarse.shape[0] * PAIR), jnp.bfloat16
        ),
        in_specs=[
            pl.BlockSpec(memory_space=pltpu.SMEM),
            pl.BlockSpec(memory_space=pltpu.VMEM),
            pl.BlockSpec(memory_space=pl.ANY),
        ],
        out_specs=pl.BlockSpec(memory_space=pltpu.VMEM),
        compiler_params=pltpu.CompilerParams(vmem_limit_bytes=4 * 1024 * 1024),
        name="pick",
    )(column_coarse, coarse, after)


def spread_cols(piece, gathered_ref, spread, right):
    n, fine_cols = gathered_ref.shape[0], COL_ROWS
    width = gathered_ref.shape[2]
    rows = gathered_ref.shape[1] - fine_cols
    side_width = right.shape[1]
    groups = spread.shape[0]
    cols = gathered_ref[:, rows:, 0:128].reshape(n * fine_cols, 128)
    lane, target = iota((128, width), 0), lax.rem(iota((128, width), 1), PAIR)
    for g in range(groups):
        if piece >= PAIR:
            take = lane == PAIR * g + target
        else:
            take = (target == piece * g + lane) & (lane < piece)
        spread[g] = jnp.dot(
            cols, ones_where(take), preferred_element_type=jnp.float32
        ).astype(jnp.bfloat16)
    for side in range(right.shape[0]):
        shape = (side_width, n * fine_cols)
        row, col = iota(shape, 0) + side * side_width, iota(shape, 1)
        fine, pair = lax.div(row, PAIR), lax.rem(row, PAIR)
        device, fine_from = lax.div(col, fine_cols), lax.rem(col, fine_cols)
        total = None
        for g in range(groups):
            if piece >= PAIR:
                take = (fine == fine_from) & (pair == groups * device + g)
            else:
                take = (fine == fine_from) & (device == groups * pair + g)
            term = jnp.dot(
                ones_where(take),
                spread[g, :, side * side_width : (side + 1) * side_width],
                preferred_element_type=jnp.float32,
            )
            total = term if total is None else total + term
        square = (side_width, side_width)
        same = lax.div(iota(square, 0), PAIR) == lax.div(iota(square, 1), PAIR)
        right[side] = jnp.where(same, total, 0.0).astype(jnp.bfloat16)


def fine_kernel(
    per_step, piece, picks_ref, gathered_ref, left_ref, out_ref, spread, right, half_done, done, sent
):
    owned = (gathered_ref.shape[1] - COL_ROWS) // PAIR
    side_width = right.shape[1]

    spread_cols(piece, gathered_ref, spread, right)

    def rows_of(coarse):
        owner = lax.div(coarse, owned)
        first = pl.multiple_of((coarse - owner * owned) * PAIR, PAIR)
        return gathered_ref[owner, pl.ds(first, PAIR), :]

    shape = (TEAM * PAIR, TEAM * 2 * PAIR)
    same_row = lax.div(iota(shape, 0), PAIR) == lax.div(iota(shape, 1), 2 * PAIR)
    steps = out_ref.shape[0] // per_step

    def send(step):
        at = pl.ds(step * per_step, per_step)
        return pltpu.make_async_copy(done.at[step % SLOTS], out_ref.at[at], sent.at[step % SLOTS])

    def one_step(step, carry):
        if step >= SLOTS:
            send(step - SLOTS).wait()

        for team in range(per_step // TEAM):
            chosen = []
            for u in range(TEAM):
                row = step * per_step + team * TEAM + u
                chosen += [rows_of(picks_ref[0, row]), rows_of(picks_ref[1, row])]
            first = (step * per_step + team * TEAM) * PAIR
            left = jnp.concatenate([left_ref[pl.ds(first, TEAM * PAIR), :]] * TEAM, axis=1)
            half_done[step % 2, team * TEAM * PAIR : (team + 1) * TEAM * PAIR, :] = jnp.dot(
                jnp.where(same_row, left, jnp.zeros_like(left)),
                jnp.concatenate(chosen, axis=0),
                preferred_element_type=jnp.float32,
            ).astype(jnp.bfloat16)
        for side in range(right.shape[0]):
            span = slice(side * side_width, (side + 1) * side_width)
            done[step % SLOTS, :, :, span] = jnp.dot(
                half_done[step % 2, :, span], right[side], preferred_element_type=jnp.float32
            ).reshape(per_step, PAIR, side_width)
        send(step).start()
        return carry

    for step in range(steps):
        one_step(step, 0)

    def finish(step, carry):
        send(step).wait()
        return carry

    for step in range(steps - SLOTS, steps):
        finish(step, 0)


def fine_rows_of(picks, gathered, left, piece):
    fine_rows = picks.shape[1]
    n, width = gathered.shape[0], gathered.shape[2]
    per_step = 16
    groups = max(piece, PAIR) // min(piece, PAIR)
    return pl.pallas_call(
        functools.partial(fine_kernel, per_step, piece),
        in_specs=[
            pl.BlockSpec(memory_space=pltpu.SMEM),
            pl.BlockSpec(memory_space=pltpu.VMEM),
            pl.BlockSpec(memory_space=pltpu.VMEM),
        ],
        out_specs=pl.BlockSpec(memory_space=pl.ANY),
        scratch_shapes=[
            pltpu.VMEM((groups, n * COL_ROWS, width), jnp.bfloat16),
            pltpu.VMEM((2, width // 2, width // 2), jnp.bfloat16),
            pltpu.VMEM((2, per_step * PAIR, width), jnp.bfloat16),
            pltpu.VMEM((SLOTS, per_step, PAIR, width), jnp.float32),
            pltpu.SemaphoreType.DMA((SLOTS,)),
        ],
        out_shape=jax.ShapeDtypeStruct((fine_rows, PAIR, width), jnp.float32),
        compiler_params=pltpu.CompilerParams(
            vmem_limit_bytes=16 * 1024 * 1024 + n * 256 * 1024
        ),
        name="fine_rows",
    )(picks, gathered, left)


def ring_place(chip, chips):
    rung, side = lax.div(chip, 2), lax.rem(chip, 2)
    return (1 - side) * rung + side * (chips - 1 - rung)


def chip_at(place, chips):
    place = lax.rem(place + 2 * chips, chips)
    side = lax.div(place, chips // 2)
    return (1 - side) * (2 * place) + side * (2 * (chips - 1 - place) + 1)


def exchange_kernel(
    n, block_ref, cols_ref, gathered_ref, ring_send, ring_recv, twin_send, twin_recv
):
    me = lax.axis_index("wide")
    chips = n // 2
    core = lax.rem(me, 2)
    place = ring_place(lax.div(me, 2), chips)
    twin = me + 1 - 2 * core
    ahead = 2 * chip_at(place + 1, chips) + core
    behind = 2 * chip_at(place - 1, chips) + core
    targets = (ahead, behind)
    rows, width = block_ref.shape
    fine_cols, piece = cols_ref.shape
    parts = ((0, rows // 2), (rows // 2, rows // 2 + fine_cols))
    far = chips // 2

    barrier = pltpu.get_barrier_semaphore()
    for friend in (ahead, behind, twin):
        pl.semaphore_signal(barrier, inc=1, device_id={"wide": friend}, device_id_type=MESH)
    gathered_ref[me, 0:rows, :] = block_ref[...]
    gathered_ref[me, rows:, :] = jnp.concatenate(
        [cols_ref[...], jnp.zeros((fine_cols, width - piece), jnp.bfloat16)], axis=1
    )
    pl.semaphore_wait(barrier, 3)

    def copy_of(part, source, send, recv, target):
        spot = gathered_ref.at[source, pl.ds(*parts[part])]
        return pltpu.make_async_remote_copy(
            src_ref=spot, dst_ref=spot, send_sem=send, recv_sem=recv,
            device_id={"wide": target}, device_id_type=MESH,
        )

    def ring_copy(way, dist, part, source):
        at = (way, dist - 1, part)
        return copy_of(part, source, ring_send.at[at], ring_recv.at[at], targets[way])

    def twin_copy(way, dist, part, source):
        at = (way, dist, part)
        return copy_of(part, source, twin_send.at[at], twin_recv.at[at], twin)

    sent, coming = [], []

    def start(copy):
        copy.start()
        sent.append(copy)

    def goes(way, dist, part):
        return dist < far or (dist == far and part == way)

    for turn in range(2):
        for way in range(2):
            if goes(way, 1, turn ^ way):
                start(ring_copy(way, 1, turn ^ way, me))
    for part in range(2):
        start(twin_copy(0, 0, part, me))
        coming.append(twin_copy(0, 0, part, twin))
    for dist in range(1, far + 1):
        chip_of = [chip_at(place + (dist if way else -dist), chips) for way in range(2)]
        for turn in range(2):
            arrived = []
            for way in range(2):
                part = turn ^ way
                if not goes(way, dist, part):
                    continue
                mine = 2 * chip_of[way] + core
                ring_copy(way, dist, part, mine).wait_recv()
                if goes(way, dist + 1, part):
                    start(ring_copy(way, dist + 1, part, mine))
                arrived.append((way, part, mine))
            for way, part, mine in arrived:
                start(twin_copy(way, dist, part, mine))
                coming.append(twin_copy(way, dist, part, mine + 1 - 2 * core))
    for copy in coming:
        copy.wait_recv()
    for copy in sent:
        copy.wait_send()


def exchange(block, cols, n):
    rows, width = block.shape
    far = n // 4
    total = n * (rows + COL_ROWS) * width * 2
    return pl.pallas_call(
        functools.partial(exchange_kernel, n),
        out_shape=jax.ShapeDtypeStruct((n, rows + COL_ROWS, width), jnp.bfloat16),
        in_specs=[
            pl.BlockSpec(memory_space=pltpu.VMEM),
            pl.BlockSpec(memory_space=pltpu.VMEM),
        ],
        out_specs=pl.BlockSpec(memory_space=pltpu.VMEM),
        scratch_shapes=[
            pltpu.SemaphoreType.DMA((2, far, 2)),
            pltpu.SemaphoreType.DMA((2, far, 2)),
            pltpu.SemaphoreType.DMA((2, far + 1, 2)),
            pltpu.SemaphoreType.DMA((2, far + 1, 2)),
        ],
        compiler_params=pltpu.CompilerParams(
            collective_id=0, has_side_effects=True, vmem_limit_bytes=total + 6 * 1024 * 1024
        ),
        name="exchange",
    )(block, cols)


def per_device(kernel_coarse, row_coeffs, col_coeffs, column_coarse, row_coarse):
    n = lax.axis_size("wide")
    coarse = kernel_coarse.reshape(kernel_coarse.shape[0] * PAIR, -1)
    fine_rows = row_coeffs.shape[0]
    left = row_coeffs.reshape(fine_rows, 2, PAIR, PAIR).transpose(0, 3, 1, 2)
    left = left.reshape(fine_rows * PAIR, 2 * PAIR)
    gathered = exchange(pick(column_coarse, coarse, left), col_coeffs, n)
    return fine_rows_of(row_coarse.T, gathered, left, col_coeffs.shape[1])


def solution(mesh):
    in_specs = (
        P(("groups", "wide"), None, None),
        P(("groups", "wide"), None, None),
        P("groups", "wide"),
        P("groups"),
        P(("groups", "wide"), None),
    )
    out_specs = P(("groups", "wide"), None, None)
    return jax.shard_map(
        per_device, mesh=mesh, in_specs=in_specs, out_specs=out_specs, check_vma=False
    )
```

```python
import functools

import jax
import jax.numpy as jnp
from jax import lax
from jax.experimental import pallas as pl
from jax.experimental.pallas import tpu as pltpu
from jax.sharding import PartitionSpec as P

PAIR = 32
SLOTS = 4
TEAM = 4
COL_ROWS = 16
MESH = pl.DeviceIdType.MESH


def iota(shape, dim):
    return lax.broadcasted_iota(jnp.int32, shape, dim)


def ones_where(mask):
    return jnp.where(mask, 1.0, 0.0).astype(jnp.bfloat16)


def pick_kernel(column_ref, coarse_ref, after_ref, picked_ref):
    lane_gap = iota((128, 128), 0) - iota((128, 128), 1)
    lane_group = lax.div(iota((128, 128), 1), PAIR)
    for block in range(picked_ref.shape[1] // 128):
        sources, moves = [], []
        for j in range(4):
            coarse = column_ref[4 * block + j]
            wide_block = lax.div(coarse, 4)
            offset = (coarse - 4 * wide_block - j) * PAIR
            sources.append(coarse_ref[:, pl.ds(pl.multiple_of(wide_block * 128, 128), 128)])
            moves.append(ones_where((lane_group == j) & (lane_gap == offset)))
        picked_ref[:, block * 128 : (block + 1) * 128] = jnp.dot(
            jnp.concatenate(sources, axis=1),
            jnp.concatenate(moves, axis=0),
            preferred_element_type=jnp.float32,
        ).astype(jnp.bfloat16)

def pick(column_coarse, coarse, after):
    return pl.pallas_call(
        pick_kernel,
        out_shape=jax.ShapeDtypeStruct(
            (coarse.shape[0], column_coarse.shape[0] * PAIR), jnp.bfloat16
        ),
        in_specs=[
            pl.BlockSpec(memory_space=pltpu.SMEM),
            pl.BlockSpec(memory_space=pltpu.VMEM),
            pl.BlockSpec(memory_space=pl.ANY),
        ],
        out_specs=pl.BlockSpec(memory_space=pltpu.VMEM),
        compiler_params=pltpu.CompilerParams(vmem_limit_bytes=4 * 1024 * 1024),
        name="pick",
    )(column_coarse, coarse, after)


def spread_cols(piece, gathered_ref, spread, right):
    n, fine_cols = gathered_ref.shape[0], COL_ROWS
    width = gathered_ref.shape[2]
    rows = gathered_ref.shape[1] - fine_cols
    side_width = right.shape[1]
    groups = spread.shape[0]
    cols = gathered_ref[:, rows:, 0:128].reshape(n * fine_cols, 128)
    lane, target = iota((128, width), 0), lax.rem(iota((128, width), 1), PAIR)
    for g in range(groups):
        if piece >= PAIR:
            take = lane == PAIR * g + target
        else:
            take = (target == piece * g + lane) & (lane < piece)
        spread[g] = jnp.dot(
            cols, ones_where(take), preferred_element_type=jnp.float32
        ).astype(jnp.bfloat16)
    for side in range(right.shape[0]):
        shape = (side_width, n * fine_cols)
        row, col = iota(shape, 0) + side * side_width, iota(shape, 1)
        fine, pair = lax.div(row, PAIR), lax.rem(row, PAIR)
        device, fine_from = lax.div(col, fine_cols), lax.rem(col, fine_cols)
        total = None
        for g in range(groups):
            if piece >= PAIR:
                take = (fine == fine_from) & (pair == groups * device + g)
            else:
                take = (fine == fine_from) & (device == groups * pair + g)
            term = jnp.dot(
                ones_where(take),
                spread[g, :, side * side_width : (side + 1) * side_width],
                preferred_element_type=jnp.float32,
            )
            total = term if total is None else total + term
        square = (side_width, side_width)
        same = lax.div(iota(square, 0), PAIR) == lax.div(iota(square, 1), PAIR)
        right[side] = jnp.where(same, total, 0.0).astype(jnp.bfloat16)


def fine_kernel(
    per_step, piece, picks_hbm, gathered_ref, left_ref, out_ref,
    spread, right, half_done, done, sent, picks_ref, fetched,
):
    owned = (gathered_ref.shape[1] - COL_ROWS) // PAIR
    side_width = right.shape[1]

    fetch = pltpu.make_async_copy(picks_hbm, picks_ref, fetched)
    fetch.start()
    spread_cols(piece, gathered_ref, spread, right)
    fetch.wait()

    def rows_of(coarse):
        owner = lax.div(coarse, owned)
        first = pl.multiple_of((coarse - owner * owned) * PAIR, PAIR)
        return gathered_ref[owner, pl.ds(first, PAIR), :]

    shape = (TEAM * PAIR, TEAM * 2 * PAIR)
    same_row = lax.div(iota(shape, 0), PAIR) == lax.div(iota(shape, 1), 2 * PAIR)
    steps = out_ref.shape[0] // per_step

    def send(step):
        at = pl.ds(step * per_step, per_step)
        return pltpu.make_async_copy(done.at[step % SLOTS], out_ref.at[at], sent.at[step % SLOTS])

    def one_step(step, carry):
        if step >= SLOTS:
            send(step - SLOTS).wait()

        for team in range(per_step // TEAM):
            chosen = []
            for u in range(TEAM):
                row = step * per_step + team * TEAM + u
                chosen += [rows_of(picks_ref[0, row]), rows_of(picks_ref[1, row])]
            first = (step * per_step + team * TEAM) * PAIR
            left = jnp.concatenate([left_ref[pl.ds(first, TEAM * PAIR), :]] * TEAM, axis=1)
            half_done[step % 2, team * TEAM * PAIR : (team + 1) * TEAM * PAIR, :] = jnp.dot(
                jnp.where(same_row, left, jnp.zeros_like(left)),
                jnp.concatenate(chosen, axis=0),
                preferred_element_type=jnp.float32,
            ).astype(jnp.bfloat16)
        for side in range(right.shape[0]):
            span = slice(side * side_width, (side + 1) * side_width)
            done[step % SLOTS, :, :, span] = jnp.dot(
                half_done[step % 2, :, span], right[side], preferred_element_type=jnp.float32
            ).reshape(per_step, PAIR, side_width)
        send(step).start()
        return carry

    for step in range(steps):
        one_step(step, 0)

    def finish(step, carry):
        send(step).wait()
        return carry

    for step in range(steps - SLOTS, steps):
        finish(step, 0)


def fine_rows_of(picks, gathered, left, piece):
    fine_rows = picks.shape[1]
    n, width = gathered.shape[0], gathered.shape[2]
    per_step = 16
    groups = max(piece, PAIR) // min(piece, PAIR)
    return pl.pallas_call(
        functools.partial(fine_kernel, per_step, piece),
        in_specs=[
            pl.BlockSpec(memory_space=pl.ANY),
            pl.BlockSpec(memory_space=pltpu.VMEM),
            pl.BlockSpec(memory_space=pltpu.VMEM),
        ],
        out_specs=pl.BlockSpec(memory_space=pl.ANY),
        scratch_shapes=[
            pltpu.VMEM((groups, n * COL_ROWS, width), jnp.bfloat16),
            pltpu.VMEM((2, width // 2, width // 2), jnp.bfloat16),
            pltpu.VMEM((2, per_step * PAIR, width), jnp.bfloat16),
            pltpu.VMEM((SLOTS, per_step, PAIR, width), jnp.float32),
            pltpu.SemaphoreType.DMA((SLOTS,)),
            pltpu.SMEM(picks.shape, jnp.int32),
            pltpu.SemaphoreType.DMA,
        ],
        out_shape=jax.ShapeDtypeStruct((fine_rows, PAIR, width), jnp.float32),
        compiler_params=pltpu.CompilerParams(
            vmem_limit_bytes=16 * 1024 * 1024 + n * 256 * 1024
        ),
        name="fine_rows",
    )(picks, gathered, left)


def ring_place(chip, chips):
    rung, side = lax.div(chip, 2), lax.rem(chip, 2)
    return (1 - side) * rung + side * (chips - 1 - rung)


def chip_at(place, chips):
    place = lax.rem(place + 2 * chips, chips)
    side = lax.div(place, chips // 2)
    return (1 - side) * (2 * place) + side * (2 * (chips - 1 - place) + 1)


def exchange_kernel(
    n, block_ref, cols_ref, gathered_ref, ring_send, ring_recv, twin_send, twin_recv
):
    me = lax.axis_index("wide")
    chips = n // 2
    core = lax.rem(me, 2)
    place = ring_place(lax.div(me, 2), chips)
    twin = me + 1 - 2 * core
    ahead = 2 * chip_at(place + 1, chips) + core
    behind = 2 * chip_at(place - 1, chips) + core
    targets = (ahead, behind)
    rows, width = block_ref.shape
    fine_cols, piece = cols_ref.shape
    parts = ((0, rows // 2), (rows // 2, rows // 2 + fine_cols))
    far = chips // 2

    barrier = pltpu.get_barrier_semaphore()
    for friend in (ahead, behind, twin):
        pl.semaphore_signal(barrier, inc=1, device_id={"wide": friend}, device_id_type=MESH)
    gathered_ref[me, 0:rows, :] = block_ref[...]
    gathered_ref[me, rows:, :] = jnp.concatenate(
        [cols_ref[...], jnp.zeros((fine_cols, width - piece), jnp.bfloat16)], axis=1
    )
    pl.semaphore_wait(barrier, 3)

    def copy_of(part, source, send, recv, target):
        spot = gathered_ref.at[source, pl.ds(*parts[part])]
        return pltpu.make_async_remote_copy(
            src_ref=spot, dst_ref=spot, send_sem=send, recv_sem=recv,
            device_id={"wide": target}, device_id_type=MESH,
        )

    def ring_copy(way, dist, part, source):
        at = (way, dist - 1, part)
        return copy_of(part, source, ring_send.at[at], ring_recv.at[at], targets[way])

    def twin_copy(way, dist, part, source):
        at = (way, dist, part)
        return copy_of(part, source, twin_send.at[at], twin_recv.at[at], twin)

    sent, coming = [], []

    def start(copy):
        copy.start()
        sent.append(copy)

    def goes(way, dist, part):
        return dist < far or (dist == far and part == way)

    for turn in range(2):
        for way in range(2):
            if goes(way, 1, turn ^ way):
                start(ring_copy(way, 1, turn ^ way, me))
    for part in range(2):
        start(twin_copy(0, 0, part, me))
        coming.append(twin_copy(0, 0, part, twin))
    for dist in range(1, far + 1):
        chip_of = [chip_at(place + (dist if way else -dist), chips) for way in range(2)]
        for turn in range(2):
            arrived = []
            for way in range(2):
                part = turn ^ way
                if not goes(way, dist, part):
                    continue
                mine = 2 * chip_of[way] + core
                ring_copy(way, dist, part, mine).wait_recv()
                if goes(way, dist + 1, part):
                    start(ring_copy(way, dist + 1, part, mine))
                arrived.append((way, part, mine))
            for way, part, mine in arrived:
                start(twin_copy(way, dist, part, mine))
                coming.append(twin_copy(way, dist, part, mine + 1 - 2 * core))
    for copy in coming:
        copy.wait_recv()
    for copy in sent:
        copy.wait_send()


def exchange(block, cols, n):
    rows, width = block.shape
    far = n // 4
    total = n * (rows + COL_ROWS) * width * 2
    return pl.pallas_call(
        functools.partial(exchange_kernel, n),
        out_shape=jax.ShapeDtypeStruct((n, rows + COL_ROWS, width), jnp.bfloat16),
        in_specs=[
            pl.BlockSpec(memory_space=pltpu.VMEM),
            pl.BlockSpec(memory_space=pltpu.VMEM),
        ],
        out_specs=pl.BlockSpec(memory_space=pltpu.VMEM),
        scratch_shapes=[
            pltpu.SemaphoreType.DMA((2, far, 2)),
            pltpu.SemaphoreType.DMA((2, far, 2)),
            pltpu.SemaphoreType.DMA((2, far + 1, 2)),
            pltpu.SemaphoreType.DMA((2, far + 1, 2)),
        ],
        compiler_params=pltpu.CompilerParams(
            collective_id=0, has_side_effects=True, vmem_limit_bytes=total + 6 * 1024 * 1024
        ),
        name="exchange",
    )(block, cols)


def per_device(kernel_coarse, row_coeffs, col_coeffs, column_coarse, row_coarse):
    n = lax.axis_size("wide")
    coarse = kernel_coarse.reshape(kernel_coarse.shape[0] * PAIR, -1)
    fine_rows = row_coeffs.shape[0]
    left = row_coeffs.reshape(fine_rows, 2, PAIR, PAIR).transpose(0, 3, 1, 2)
    left = left.reshape(fine_rows * PAIR, 2 * PAIR)
    gathered = exchange(pick(column_coarse, coarse, left), col_coeffs, n)
    return fine_rows_of(row_coarse.T, gathered, left, col_coeffs.shape[1])


def solution(mesh):
    in_specs = (
        P(("groups", "wide"), None, None),
        P(("groups", "wide"), None, None),
        P("groups", "wide"),
        P("groups"),
        P(("groups", "wide"), None),
    )
    out_specs = P(("groups", "wide"), None, None)
    return jax.shard_map(
        per_device, mesh=mesh, in_specs=in_specs, out_specs=out_specs, check_vma=False
    )
```
